32 devices in a mesh: dp: 4 (over y, core), tensor: 8 (over z, x).
Axes of the slice: x: 2, y: 2, z: 4, core: 2. Of those that a mesh axis runs over, the one named last changes fastest.
Arguments:
- tokens: bfloat16 [4096, 1024], P(('dp', 'tensor')), may hold values from -6 to 6
- doc_lengths: int32 [4, 3], P('dp'), may hold values from 1 to 512, 1024 in all within a row
- attn_gain: bfloat16 [1024], P('dp'), may hold values from 0.25 to 1.75
- qkv_weight: bfloat16 [1024, 3, 1024], P('dp', None, 'tensor'), may hold values from -0.1875 to 0.1875
- proj_weight: bfloat16 [1024, 1024], P('tensor', 'dp'), may hold values from -0.75 to 0.75
- mlp_gain: bfloat16 [1024], P('dp'), may hold values from 0.25 to 1.75
- in_weight: bfloat16 [1024, 2, 2624], P('dp', None, 'tensor'), may hold values from -0.1875 to 0.1875
- out_weight: bfloat16 [2624, 1024], P('tensor', 'dp'), may hold values from -0.125 to 0.125
- cotangent: bfloat16 [4096, 1024], P(('dp', 'tensor')), may hold values from -6 to 6
Outputs:
- block_out: bfloat16 [4096, 1024], P(('dp', 'tensor'))
- tokens_grad: bfloat16 [4096, 1024], P(('dp', 'tensor'))
- attn_gain_grad: float32 [1024], P('dp')
- qkv_weight_grad: float32 [1024, 3, 1024], P('dp', None, 'tensor')
- proj_weight_grad: float32 [1024, 1024], P('tensor', 'dp')
- mlp_gain_grad: float32 [1024], P('dp')
- in_weight_grad: float32 [1024, 2, 2624], P('dp', None, 'tensor')
- out_weight_grad: float32 [2624, 1024], P('tensor', 'dp')
The draws below stay inside these ranges and needn't reach their ends.
Inputs may be any that keep to these rules, and one draw needn't show every extreme that they name: `doc_lengths`: row g holds, in order, the lengths of the 3 documents packed into pack g; they sum to 1024 and the longest is exactly 512.
All inputs are finite; a program needn't handle non-finite values.
Results may differ from the reference program's by a relative error of at most 0.025.
Values may be sent and summed in bfloat16 or wider, within the bound.
A program may use at most 128 MiB of HBM per device.

```python
import math
import jax
import jax.numpy as jnp
import numpy as np
from jax import lax

D = 1024
HEADS = 16
HEAD_DIM = 64
FF = 2624
GROUP = 1024
DOC_MOST = 512
DOCS = 3
TOKENS = 4096
N_DP = 4


def block_levels(stream_key, shape, cuts, low, largest):
    level, own = 1.0, jax.random.fold_in(stream_key, 6)
    for dim, shards_of in cuts:
        heights = jnp.exp(jax.random.uniform(jax.random.fold_in(own, dim), (shards_of,), jnp.float32, low / len(cuts), largest / len(cuts)))
        level = level * jnp.repeat(heights, shape[dim] // shards_of).reshape([-1 if axis == dim else 1 for axis in range(len(shape))])
    return level


def length_profile(count, total, most, slope):
    portions = [(1 << 20) // math.isqrt(grade ** slope) + 1 for grade in range(2, count + 1)]
    spare, holding = total - most - (count - 1), [1] * (count - 1)
    while spare > 0:
        candidates = [i for i in range(count - 1) if holding[i] < most]
        whole, budget = sum([portions[i] for i in candidates]), spare
        for i in candidates:
            addition = min(most - holding[i], max(1, budget * portions[i] // whole), spare)
            holding[i] = holding[i] + addition
            spare = spare - addition
    return np.array([most] + holding)


def ragged_sizes(own_key, count, total, most, skew):
    if count == 2:
        one = jax.random.randint(own_key, (), max(1, total - most), min(most, total - 1) + 1)
        return jnp.stack([one, total - one])
    sizes = jnp.asarray(length_profile(count, total, most, skew), jnp.int32)
    twos = (count - 1) // 2
    giver, sink = sizes[1:1 + 2 * twos:2], sizes[2:2 + 2 * twos:2]
    room = jnp.minimum(giver - 1, most - sink)
    passed = jax.random.randint(jax.random.fold_in(own_key, 1), (twos,), 0, 1 << 20) % (room + 1)
    sizes = sizes.at[1:1 + 2 * twos:2].set(giver - passed).at[2:2 + 2 * twos:2].set(sink + passed)
    return sizes[jax.random.permutation(jax.random.fold_in(own_key, 2), count)]


def normal_values(key, extent, scale, limit, cuts=(), kind=jnp.bfloat16):
    loudness = block_levels(key, extent, cuts, -0.22, 0.18) if cuts else 1.0
    values = jax.random.normal(key, extent, jnp.float32) * scale * loudness
    return jnp.minimum(jnp.maximum(values, -limit), limit).astype(kind)


def setup_inputs(seed: int = 0) -> dict:
    key_of = jax.random.split(jax.random.key(seed), 10)
    tokens = normal_values(key_of[0], (TOKENS, D), 1.0, 6.0, ((0, 32),))
    doc_lengths = jax.vmap(lambda own: ragged_sizes(own, DOCS, GROUP, DOC_MOST, 1))(jax.random.split(key_of[1], N_DP)).reshape((N_DP, DOCS)).astype(jnp.int32)
    attn_gain = jnp.clip(1.0 + 0.15 * jax.random.normal(key_of[2], (D,), jnp.float32), 0.25, 1.75).astype(jnp.bfloat16)
    qkv_weight = normal_values(key_of[3], (D, 3, D), D ** -0.5, 0.1875, ((0, 4), (2, 8)))
    proj_weight = normal_values(key_of[4], (D, D), HEAD_DIM ** -0.5, 0.75, ((0, 8), (1, 4)))
    mlp_gain = jnp.clip(1.0 + 0.15 * jax.random.normal(key_of[5], (D,), jnp.float32), 0.25, 1.75).astype(jnp.bfloat16)
    in_weight = normal_values(key_of[6], (D, 2, FF), D ** -0.5, 0.1875, ((0, 4), (2, 8)))
    out_weight = normal_values(key_of[7], (FF, D), FF ** -0.5, 0.125, ((0, 8), (1, 4)))
    cotangent = normal_values(key_of[8], (TOKENS, D), 1.0, 6.0, ((0, 32),))
    return {"tokens": tokens, "doc_lengths": doc_lengths, "attn_gain": attn_gain, "qkv_weight": qkv_weight, "proj_weight": proj_weight, "mlp_gain": mlp_gain, "in_weight": in_weight, "out_weight": out_weight, "cotangent": cotangent}


EPSILON = 1e-05
ROPE_BASE = 160000.0
MASKED = -1000000000.0
HIGHEST = lax.Precision.HIGHEST

@jax.custom_vjp
def low(v):
    return lax.optimization_barrier(v.astype(jnp.bfloat16)).astype(jnp.float32)

@jax.custom_vjp
def low_back(v):
    return v

def low_keep(v):
    return (low(v), None)

def low_pass(kept, grad):
    return (grad,)

def back_keep(v):
    return (v, None)

def back_low(kept, grad):
    return (low(grad),)
low.defvjp(low_keep, low_pass)
low_back.defvjp(back_keep, back_low)

def layer_norm(values):
    centered = values - lax.optimization_barrier(jnp.mean(values, axis=-1, keepdims=True))
    spread = lax.optimization_barrier(jnp.mean(centered * centered, axis=-1, keepdims=True))
    return centered * lax.rsqrt(spread + EPSILON)

def rotary_tables(amount, head_width):
    half_width = head_width // 2
    frequency = jnp.exp(jnp.arange(half_width, dtype=jnp.float32) * (-2.0 * math.log(ROPE_BASE) / head_width))
    angles = jnp.arange(amount, dtype=jnp.float32)[:, None] * frequency[None, :]
    return (jnp.cos(angles), jnp.sin(angles))

def rotate(values, cosine, sine):
    half_width = values.shape[-1] // 2
    lower_half = values[..., :half_width]
    upper_half = values[..., half_width:]
    cos_rows = cosine[:, None, :]
    sin_rows = sine[:, None, :]
    return jnp.concatenate([lower_half * cos_rows - upper_half * sin_rows, upper_half * cos_rows + lower_half * sin_rows], axis=-1)

def documents(lengths, amount):
    doc_ends = jnp.cumsum(lengths.astype(jnp.int32)).astype(jnp.int32)
    positions = jnp.arange(amount, dtype=jnp.int32)
    return lax.optimization_barrier(jnp.sum((positions[:, None] >= doc_ends[None, :]).astype(jnp.int32), axis=1))

def attend_group(packed):
    qkv_rows, lengths = packed
    amount = qkv_rows.shape[0]
    split_rows = qkv_rows.reshape(amount, 3, HEADS, HEAD_DIM)
    cosine, sine = rotary_tables(amount, HEAD_DIM)
    queries = low(rotate(split_rows[:, 0], cosine, sine))
    key_rows = low(rotate(split_rows[:, 1], cosine, sine))
    values = low(split_rows[:, 2])
    scores = jnp.einsum('qhd,khd->hqk', queries, key_rows, precision=HIGHEST) / math.sqrt(HEAD_DIM)
    scores = low_back(scores)
    doc_ids = documents(lengths, amount)
    same_doc = doc_ids[:, None] == doc_ids[None, :]
    scores = jnp.where(same_doc[None], scores, MASKED)
    row_top = lax.optimization_barrier(jnp.max(scores, axis=-1, keepdims=True))
    exp_scores = jnp.exp(scores - row_top)
    weights = low(exp_scores / lax.optimization_barrier(jnp.sum(exp_scores, axis=-1, keepdims=True)))
    attended = jnp.einsum('hqk,khd->qhd', weights, values, precision=HIGHEST)
    return attended.reshape(amount, HEADS * HEAD_DIM)

def forward(tokens, attn_gain, qkv_weight, proj_weight, mlp_gain, in_weight, out_weight, doc_lengths):
    attn_normed = low(layer_norm(tokens) * attn_gain)
    qkv_rows = low_back(jnp.dot(attn_normed, qkv_weight.reshape(D, 3 * D), precision=HIGHEST))
    packs = qkv_rows.reshape(N_DP, GROUP, 3 * D)
    attended = lax.map(jax.checkpoint(attend_group), (packs, doc_lengths))
    attended = low(low_back(attended.reshape(N_DP * GROUP, D)))
    attn_branch = low_back(jnp.dot(attended, proj_weight, precision=HIGHEST))
    residual = tokens + attn_branch
    mlp_normed = low(layer_norm(residual) * mlp_gain)
    projected = low_back(jnp.dot(mlp_normed, in_weight.reshape(D, 2 * FF), precision=HIGHEST))
    hidden = low(jax.nn.gelu(projected[:, :FF], approximate=False) * projected[:, FF:])
    mlp_branch = low_back(jnp.dot(hidden, out_weight, precision=HIGHEST))
    return residual + mlp_branch

def reference(tokens, doc_lengths, attn_gain, qkv_weight, proj_weight, mlp_gain, in_weight, out_weight, cotangent):

    def forward_only(*inputs_all):
        return forward(*inputs_all, doc_lengths)
    inputs_all = tuple((a.astype(jnp.float32) for a in (tokens, attn_gain, qkv_weight, proj_weight, mlp_gain, in_weight, out_weight)))
    block_out, pullback = jax.vjp(forward_only, *inputs_all)
    gradient = pullback(cotangent.astype(jnp.float32))
    return (block_out.astype(jnp.bfloat16), gradient[0].astype(jnp.bfloat16), gradient[1], gradient[2], gradient[3], gradient[4], gradient[5], gradient[6])
```

```python
import functools
import math

import jax
import jax.numpy as jnp
from jax import lax
from jax.experimental import pallas as pl
from jax.experimental.pallas import tpu as pltpu
from jax.sharding import PartitionSpec as P

HEAD_DIM = 64


EPSILON = 1e-05
ROPE_BASE = 160000.0
MASKED = -1000000000.0


def layer_norm(values):
    centered = values - jnp.mean(values, axis=-1, keepdims=True)
    spread = jnp.mean(centered * centered, axis=-1, keepdims=True)
    inverse = lax.rsqrt(spread + EPSILON)
    return (centered * inverse, inverse)


def norm_back(scaled_grad, plain_rows, inverse):
    first_mean = jnp.mean(scaled_grad, axis=-1, keepdims=True)
    second_mean = jnp.mean(scaled_grad * plain_rows, axis=-1, keepdims=True)
    return inverse * (scaled_grad - first_mean - plain_rows * second_mean)


def rotary_tables(amount, head_width):
    half_width = head_width // 2
    frequency = jnp.exp(
        jnp.arange(half_width, dtype=jnp.float32) * (-2.0 * math.log(ROPE_BASE) / head_width)
    )
    angles = jnp.arange(amount, dtype=jnp.float32)[:, None] * frequency[None, :]
    return (jnp.cos(angles), jnp.sin(angles))


def rotate(values, cosine, sine):
    half_width = values.shape[-1] // 2
    lower_half = values[..., :half_width]
    upper_half = values[..., half_width:]
    cos_rows = cosine[:, None, :]
    sin_rows = sine[:, None, :]
    return jnp.concatenate(
        [
            lower_half * cos_rows - upper_half * sin_rows,
            upper_half * cos_rows + lower_half * sin_rows,
        ],
        axis=-1,
    )


def unrotate(gradient, cosine, sine):
    half_width = gradient.shape[-1] // 2
    lower_half = gradient[..., :half_width]
    upper_half = gradient[..., half_width:]
    cos_rows = cosine[:, None, :]
    sin_rows = sine[:, None, :]
    return jnp.concatenate(
        [
            lower_half * cos_rows + upper_half * sin_rows,
            upper_half * cos_rows - lower_half * sin_rows,
        ],
        axis=-1,
    )


def documents(lengths, amount):
    doc_ends = jnp.cumsum(lengths)
    positions = jnp.arange(amount, dtype=jnp.int32)
    return jnp.sum((positions[:, None] >= doc_ends[None, :]).astype(jnp.int32), axis=1)


def exact_gelu(values):
    return jax.nn.gelu(values, approximate=False)


def contract_last(left_side, right_side):
    return lax.dot_general(
        left_side, right_side, (((1,), (1,)), ((), ())), preferred_element_type=jnp.float32
    )


def contract_first(left_side, right_side):
    return lax.dot_general(
        left_side, right_side, (((0,), (0,)), ((), ())), preferred_element_type=jnp.float32
    )


VMEM_GRANT = 48 * 1024 * 1024


def enter(axis, amount):
    me = lax.axis_index(axis)
    partner = me + 1 - 2 * lax.rem(me, 2)
    peers = [lax.rem(me + 2 * step, amount) for step in range(1, amount // 2)]
    barrier = pltpu.get_barrier_semaphore()
    for other in [partner] + peers:
        pl.semaphore_signal(
            barrier, inc=1, device_id={axis: other}, device_id_type=pl.DeviceIdType.MESH
        )
    pl.semaphore_wait(barrier, amount // 2)
    return (me, partner)


def remote(source, target, send_sem, recv_sem, axis, other):
    return pltpu.make_async_remote_copy(
        src_ref=source,
        dst_ref=target,
        send_sem=send_sem,
        recv_sem=recv_sem,
        device_id={axis: other},
        device_id_type=pl.DeviceIdType.MESH,
    )


def gather_kernel(axis, amount, x_ref, o_ref, send_peer, recv_peer, send_pair, recv_pair, own_sem):
    me, partner = enter(axis, amount)
    half = amount // 2
    own = pltpu.make_async_copy(x_ref, o_ref.at[me], own_sem)
    own.start()
    pair = [remote(x_ref, o_ref.at[me], send_pair.at[0], recv_pair.at[0], axis, partner)]
    pair[0].start()
    peer = [None]
    for step in range(1, half):
        other = lax.rem(me + 2 * step, amount)
        copy = remote(x_ref, o_ref.at[me], send_peer.at[step], recv_peer.at[step], axis, other)
        copy.start()
        peer.append(copy)
    for step in range(1, half):
        origin = lax.rem(me + amount - 2 * step, amount)
        peer[step].wait_recv()
        copy = remote(
            o_ref.at[origin],
            o_ref.at[origin],
            send_pair.at[step],
            recv_pair.at[step],
            axis,
            partner,
        )
        copy.start()
        pair.append(copy)
    for step in range(half):
        pair[step].wait_recv()
    own.wait()
    for step in range(half):
        pair[step].wait_send()
        if step:
            peer[step].wait_send()


def gather_rows(rows, axis, collective_id):
    amount = lax.axis_size(axis)
    half = amount // 2
    count, width = rows.shape
    gathered = pl.pallas_call(
        functools.partial(gather_kernel, axis, amount),
        out_shape=jax.ShapeDtypeStruct((amount, count, width), rows.dtype),
        in_specs=[pl.BlockSpec(memory_space=pltpu.VMEM)],
        out_specs=pl.BlockSpec(memory_space=pltpu.VMEM),
        scratch_shapes=[
            pltpu.SemaphoreType.DMA((half,)),
            pltpu.SemaphoreType.DMA((half,)),
            pltpu.SemaphoreType.DMA((half,)),
            pltpu.SemaphoreType.DMA((half,)),
            pltpu.SemaphoreType.DMA,
        ],
        compiler_params=pltpu.CompilerParams(
            collective_id=collective_id, has_side_effects=True, vmem_limit_bytes=VMEM_GRANT
        ),
        cost_estimate=pl.CostEstimate(flops=40_000_000_000, bytes_accessed=0, transcendentals=0),
    )(rows)
    return gathered.reshape(amount * count, width)


def scatter_kernel(
    axis,
    amount,
    weight_dim,
    a_ref,
    w_ref,
    o_ref,
    staged,
    from_pair,
    staged_peer,
    from_peer,
    send_pair,
    recv_pair,
    send_peer,
    recv_peer,
):
    me, partner = enter(axis, amount)
    half = amount // 2
    order = list(range(1, half)) + [0]

    def product(chunk):
        return lax.dot_general(
            a_ref[chunk],
            w_ref[...],
            (((1,), (weight_dim,)), ((), ())),
            preferred_element_type=jnp.float32,
        )

    pair, peer = {}, {}
    for step in order:
        staged[step] = product(lax.rem(partner + 2 * step, amount)).astype(jnp.bfloat16)
        pair[step] = remote(
            staged.at[step],
            from_pair.at[step],
            send_pair.at[step],
            recv_pair.at[step],
            axis,
            partner,
        )
        pair[step].start()
    for step in order[:-1]:
        other = lax.rem(me + 2 * step, amount)
        own = product(other)
        pair[step].wait_recv()
        staged_peer[step] = (own + from_pair[step].astype(jnp.float32)).astype(jnp.bfloat16)
        peer[step] = remote(
            staged_peer.at[step],
            from_peer.at[step],
            send_peer.at[step],
            recv_peer.at[step],
            axis,
            other,
        )
        peer[step].start()
    own = product(me)
    pair[0].wait_recv()
    o_ref[...] = own + from_pair[0].astype(jnp.float32)
    for step in range(1, half):
        peer[step].wait_recv()
        o_ref[...] += from_peer[step].astype(jnp.float32)
    for step in order:
        pair[step].wait_send()
        if step:
            peer[step].wait_send()


def product_scatter(rows, weight, weight_dim, axis, collective_id):
    amount = lax.axis_size(axis)
    half = amount // 2
    count = rows.shape[0] // amount
    width = weight.shape[1 - weight_dim]
    slots = pltpu.VMEM((half, count, width), jnp.bfloat16)
    return pl.pallas_call(
        functools.partial(scatter_kernel, axis, amount, weight_dim),
        out_shape=jax.ShapeDtypeStruct((count, width), jnp.float32),
        in_specs=[pl.BlockSpec(memory_space=pltpu.VMEM)] * 2,
        out_specs=pl.BlockSpec(memory_space=pltpu.VMEM),
        scratch_shapes=[slots] * 4 + [pltpu.SemaphoreType.DMA((half,))] * 4,
        compiler_params=pltpu.CompilerParams(
            collective_id=collective_id, has_side_effects=True, vmem_limit_bytes=VMEM_GRANT
        ),
        cost_estimate=pl.CostEstimate(flops=40_000_000_000, bytes_accessed=0, transcendentals=0),
    )(rows.reshape(amount, count, rows.shape[1]), weight)


def body(
    tokens,
    doc_lengths,
    attn_gain,
    qkv_weight,
    proj_weight,
    mlp_gain,
    in_weight,
    out_weight,
    cotangent,
):
    gathered = (
        lax.all_gather(attn_gain, "dp", axis=0, tiled=True),
        lax.all_gather(qkv_weight, "dp", axis=0, tiled=True),
        lax.all_gather(proj_weight, "dp", axis=1, tiled=True),
        lax.all_gather(mlp_gain, "dp", axis=0, tiled=True),
        lax.all_gather(in_weight, "dp", axis=0, tiled=True),
        lax.all_gather(out_weight, "dp", axis=1, tiled=True),
    )
    attn_scale = gathered[0].astype(jnp.float32)
    qkv_full = gathered[1]
    proj_local = gathered[2]
    mlp_scale = gathered[3].astype(jnp.float32)
    in_full = gathered[4]
    out_rows = gathered[5]
    model_width = qkv_full.shape[0]
    local_width = qkv_full.shape[2]
    local_heads = local_width // HEAD_DIM
    local_units = in_full.shape[2]
    qkv_mat = qkv_full.reshape(model_width, 3 * local_width)
    in_mat = in_full.reshape(model_width, 2 * local_units)
    row_count = tokens.shape[0]
    group_rows = row_count * lax.axis_size("tensor")
    block_rows = min(512, group_rows)
    block_count = group_rows // block_rows
    score_scale = 1.0 / math.sqrt(HEAD_DIM)
    cosine, sine = rotary_tables(group_rows, HEAD_DIM)
    doc_ids = documents(doc_lengths[0], group_rows)
    inputs = tokens.astype(jnp.float32)
    plain_one, inverse_one = layer_norm(inputs)
    attn_normed = (plain_one * attn_scale).astype(jnp.bfloat16)
    attn_all = gather_rows(attn_normed, "tensor", 1)
    qkv_rows = jnp.dot(attn_all, qkv_mat, preferred_element_type=jnp.float32).reshape(
        group_rows, 3, local_heads, HEAD_DIM
    )
    queries = rotate(qkv_rows[:, 0], cosine, sine).astype(jnp.bfloat16)
    key_rows = rotate(qkv_rows[:, 1], cosine, sine).astype(jnp.bfloat16)
    values = qkv_rows[:, 2].astype(jnp.bfloat16)

    def block_scores(offset):
        query_rows = lax.dynamic_slice_in_dim(queries, offset, block_rows, 0)
        scores = (
            jnp.einsum("qhd,khd->hqk", query_rows, key_rows, preferred_element_type=jnp.float32)
            * score_scale
        )
        block_ids = lax.dynamic_slice_in_dim(doc_ids, offset, block_rows, 0)
        same_doc = block_ids[:, None] == doc_ids[None, :]
        return (jnp.where(same_doc[None], scores, MASKED), query_rows)

    def forward_block(block_index):
        scores, query_rows = block_scores(block_index * block_rows)
        row_top = jnp.max(scores, axis=-1, keepdims=True)
        exp_scores = jnp.exp(scores - row_top)
        row_total = jnp.sum(exp_scores, axis=-1, keepdims=True)
        weights = (exp_scores / row_total).astype(jnp.bfloat16)
        result = jnp.einsum("hqk,khd->qhd", weights, values, preferred_element_type=jnp.float32)
        return (
            result.astype(jnp.bfloat16).reshape(block_rows, local_width),
            (row_top + jnp.log(row_total))[..., 0],
        )

    attended, logsum = lax.map(forward_block, jnp.arange(block_count))
    attended = attended.reshape(group_rows, local_width)
    attn_branch = product_scatter(attended, proj_local, 0, "tensor", 5)
    residual = inputs + attn_branch
    plain_two, inverse_two = layer_norm(residual)
    mlp_normed = (plain_two * mlp_scale).astype(jnp.bfloat16)
    mlp_all = gather_rows(mlp_normed, "tensor", 2)
    projected = jnp.dot(mlp_all, in_mat, preferred_element_type=jnp.float32)
    inner_part = projected[:, :local_units]
    gate_part = projected[:, local_units:]
    activated, gelu_pull = jax.vjp(exact_gelu, inner_part)
    hidden = (activated * gate_part).astype(jnp.bfloat16)
    mlp_branch = product_scatter(hidden, out_rows, 0, "tensor", 6)
    block_out = (residual + mlp_branch).astype(jnp.bfloat16)
    out_cot = cotangent.astype(jnp.float32)
    out_low = out_cot.astype(jnp.bfloat16)
    out_all = gather_rows(out_low, "tensor", 3)
    out_weight_grad = contract_first(hidden, out_all)
    hidden_grad = contract_last(out_all, out_rows)
    inner_grad = gelu_pull(hidden_grad * gate_part)[0]
    gate_grad = hidden_grad * activated
    projected_grad = jnp.concatenate([inner_grad, gate_grad], axis=1).astype(jnp.bfloat16)
    in_weight_grad = contract_first(mlp_all, projected_grad).reshape(model_width, 2, local_units)
    mlp_normed_grad = product_scatter(projected_grad, in_mat, 1, "tensor", 7)
    mlp_gain_part = jnp.sum(mlp_normed_grad * plain_two, axis=0)
    residual_grad = out_cot + norm_back(mlp_normed_grad * mlp_scale, plain_two, inverse_two)
    residual_low = residual_grad.astype(jnp.bfloat16)
    branch_all = gather_rows(residual_low, "tensor", 4)
    proj_weight_grad = contract_first(attended, branch_all)
    attended_grad = (
        contract_last(branch_all, proj_local)
        .astype(jnp.bfloat16)
        .reshape(group_rows, local_heads, HEAD_DIM)
    )

    def backward_block(totals, block_index):
        key_total, value_total = totals
        offset = block_index * block_rows
        scores, query_rows = block_scores(offset)
        weights = jnp.exp(scores - logsum[block_index][..., None])
        grad_rows = lax.dynamic_slice_in_dim(attended_grad, offset, block_rows, 0)
        value_total = value_total + jnp.einsum(
            "hqk,qhd->khd",
            weights.astype(jnp.bfloat16),
            grad_rows,
            preferred_element_type=jnp.float32,
        )
        weight_grad = jnp.einsum(
            "qhd,khd->hqk", grad_rows, values, preferred_element_type=jnp.float32
        )
        delta = jnp.sum(weights * weight_grad, axis=-1, keepdims=True)
        score_grad = (weights * (weight_grad - delta)).astype(jnp.bfloat16)
        query_grad = (
            jnp.einsum("hqk,khd->qhd", score_grad, key_rows, preferred_element_type=jnp.float32)
            * score_scale
        )
        key_total = (
            key_total
            + jnp.einsum("hqk,qhd->khd", score_grad, query_rows, preferred_element_type=jnp.float32)
            * score_scale
        )
        return ((key_total, value_total), query_grad)

    zeros_head = jnp.zeros((group_rows, local_heads, HEAD_DIM), jnp.float32)
    (key_grad, value_grad), query_grad = lax.scan(
        backward_block, (zeros_head, zeros_head), jnp.arange(block_count)
    )
    query_grad = query_grad.reshape(group_rows, local_heads, HEAD_DIM)
    qkv_low_grad = jnp.stack(
        [unrotate(query_grad, cosine, sine), unrotate(key_grad, cosine, sine), value_grad], axis=1
    )
    qkv_low_grad = qkv_low_grad.astype(jnp.bfloat16).reshape(group_rows, 3 * local_width)
    qkv_weight_grad = contract_first(attn_all, qkv_low_grad).reshape(model_width, 3, local_width)
    attn_normed_grad = product_scatter(qkv_low_grad, qkv_mat, 1, "tensor", 8)
    attn_gain_part = jnp.sum(attn_normed_grad * plain_one, axis=0)
    tokens_grad = (
        residual_grad + norm_back(attn_normed_grad * attn_scale, plain_one, inverse_one)
    ).astype(jnp.bfloat16)
    summed = (
        lax.psum_scatter(
            attn_gain_part.astype(jnp.bfloat16), "dp", scatter_dimension=0, tiled=True
        ).astype(jnp.float32),
        lax.psum_scatter(
            qkv_weight_grad.astype(jnp.bfloat16), "dp", scatter_dimension=0, tiled=True
        ).astype(jnp.float32),
        lax.psum_scatter(
            proj_weight_grad.astype(jnp.bfloat16), "dp", scatter_dimension=1, tiled=True
        ).astype(jnp.float32),
        lax.psum_scatter(
            mlp_gain_part.astype(jnp.bfloat16), "dp", scatter_dimension=0, tiled=True
        ).astype(jnp.float32),
        lax.psum_scatter(
            in_weight_grad.astype(jnp.bfloat16), "dp", scatter_dimension=0, tiled=True
        ).astype(jnp.float32),
        lax.psum_scatter(
            out_weight_grad.astype(jnp.bfloat16), "dp", scatter_dimension=1, tiled=True
        ).astype(jnp.float32),
    )
    attn_gain_grad, mlp_gain_grad = lax.psum((summed[0], summed[3]), "tensor")
    return (
        block_out,
        tokens_grad,
        attn_gain_grad,
        summed[1],
        summed[2],
        mlp_gain_grad,
        summed[4],
        summed[5],
    )


def solution(mesh):
    in_specs = (
        P(("dp", "tensor"), None),
        P("dp", None),
        P("dp"),
        P("dp", None, "tensor"),
        P("tensor", "dp"),
        P("dp"),
        P("dp", None, "tensor"),
        P("tensor", "dp"),
        P(("dp", "tensor"), None),
    )
    out_specs = (
        P(("dp", "tensor"), None),
        P(("dp", "tensor"), None),
        P("dp"),
        P("dp", None, "tensor"),
        P("tensor", "dp"),
        P("dp"),
        P("dp", None, "tensor"),
        P("tensor", "dp"),
    )
    return jax.shard_map(body, mesh=mesh, in_specs=in_specs, out_specs=out_specs, check_vma=False)
```

```python
import functools
import math

import jax
import jax.numpy as jnp
from jax import lax
from jax.experimental import pallas as pl
from jax.experimental.pallas import tpu as pltpu
from jax.sharding import PartitionSpec as P

HEAD_DIM = 64


EPSILON = 1e-05
ROPE_BASE = 160000.0
MASKED = -1000000000.0


def layer_norm(values):
    centered = values - jnp.mean(values, axis=-1, keepdims=True)
    spread = jnp.mean(centered * centered, axis=-1, keepdims=True)
    inverse = lax.rsqrt(spread + EPSILON)
    return (centered * inverse, inverse)


def norm_back(scaled_grad, plain_rows, inverse):
    first_mean = jnp.mean(scaled_grad, axis=-1, keepdims=True)
    second_mean = jnp.mean(scaled_grad * plain_rows, axis=-1, keepdims=True)
    return inverse * (scaled_grad - first_mean - plain_rows * second_mean)


def rotary_tables(amount, head_width):
    half_width = head_width // 2
    frequency = jnp.exp(
        jnp.arange(half_width, dtype=jnp.float32) * (-2.0 * math.log(ROPE_BASE) / head_width)
    )
    angles = jnp.arange(amount, dtype=jnp.float32)[:, None] * frequency[None, :]
    return (jnp.cos(angles), jnp.sin(angles))


def rotate(values, cosine, sine):
    half_width = values.shape[-1] // 2
    lower_half = values[..., :half_width]
    upper_half = values[..., half_width:]
    cos_rows = cosine[:, None, :]
    sin_rows = sine[:, None, :]
    return jnp.concatenate(
        [
            lower_half * cos_rows - upper_half * sin_rows,
            upper_half * cos_rows + lower_half * sin_rows,
        ],
        axis=-1,
    )


def unrotate(gradient, cosine, sine):
    half_width = gradient.shape[-1] // 2
    lower_half = gradient[..., :half_width]
    upper_half = gradient[..., half_width:]
    cos_rows = cosine[:, None, :]
    sin_rows = sine[:, None, :]
    return jnp.concatenate(
        [
            lower_half * cos_rows + upper_half * sin_rows,
            upper_half * cos_rows - lower_half * sin_rows,
        ],
        axis=-1,
    )


def documents(lengths, amount):
    doc_ends = jnp.cumsum(lengths)
    positions = jnp.arange(amount, dtype=jnp.int32)
    return jnp.sum((positions[:, None] >= doc_ends[None, :]).astype(jnp.int32), axis=1)


def exact_gelu(values):
    return jax.nn.gelu(values, approximate=False)


def contract_last(left_side, right_side):
    return lax.dot_general(
        left_side, right_side, (((1,), (1,)), ((), ())), preferred_element_type=jnp.float32
    )


def contract_first(left_side, right_side):
    return lax.dot_general(
        left_side, right_side, (((0,), (0,)), ((), ())), preferred_element_type=jnp.float32
    )


VMEM_GRANT = 48 * 1024 * 1024


def remote(source, target, sems, step, axis, other):
    return pltpu.make_async_remote_copy(
        src_ref=source,
        dst_ref=target,
        send_sem=sems[0].at[step],
        recv_sem=sems[1].at[step],
        device_id={axis: other},
        device_id_type=pl.DeviceIdType.MESH,
    )


def place(axis, amount):
    me = lax.axis_index(axis)
    return (me, me + 1 - 2 * lax.rem(me, 2))


def greet(axes):
    barrier = pltpu.get_barrier_semaphore()
    total = 0
    for axis, amount in axes:
        me, partner = place(axis, amount)
        peers = [lax.rem(me + 2 * step, amount) for step in range(1, amount // 2)]
        for other in [partner] + peers:
            pl.semaphore_signal(
                barrier, inc=1, device_id={axis: other}, device_id_type=pl.DeviceIdType.MESH
            )
        total += amount // 2
    pl.semaphore_wait(barrier, total)


def steps_by_distance(half):
    return sorted(range(1, half), key=lambda step: min(step, half - step))


def gather_steps(axis, amount, x_ref, o_ref, peer_sems, pair_sems, own_sem):
    me, partner = place(axis, amount)
    half = amount // 2
    order = steps_by_distance(half)
    own = pltpu.make_async_copy(x_ref, o_ref.at[me], own_sem)
    own.start()
    pair = [remote(x_ref, o_ref.at[me], pair_sems, 0, axis, partner)]
    peer = [
        remote(x_ref, o_ref.at[me], peer_sems, step, axis, lax.rem(me + 2 * step, amount))
        for step in order
    ]
    peer[0].start()
    pair[0].start()
    if half > 2:
        peer[1].start()
    yield
    for index, step in enumerate(order):
        origin = lax.rem(me + amount - 2 * step, amount)
        peer[index].wait_recv()
        pair.append(remote(o_ref.at[origin], o_ref.at[origin], pair_sems, step, axis, partner))
        pair[-1].start()
        peer[index].wait_send()
        if index + 2 < half - 1:
            peer[index + 2].start()
        yield
    for copy in pair:
        copy.wait_recv()
    own.wait()
    for copy in pair:
        copy.wait_send()


def scatter_steps(
    axis,
    amount,
    weight_dim,
    a_ref,
    w_ref,
    o_ref,
    staged,
    from_pair,
    staged_peer,
    from_peer,
    pair_sems,
    peer_sems,
):
    me, partner = place(axis, amount)
    half = amount // 2
    order = steps_by_distance(half)[::-1] + [0]

    def product(chunk):
        if w_ref is None:
            return a_ref[chunk].astype(jnp.float32)
        return lax.dot_general(
            a_ref[chunk],
            w_ref[...],
            (((1,), (weight_dim,)), ((), ())),
            preferred_element_type=jnp.float32,
        )

    def send_pair(step):
        chunk = lax.rem(partner + 2 * step, amount)
        if w_ref is None:
            source = a_ref.at[chunk]
        else:
            staged[step] = product(chunk).astype(jnp.bfloat16)
            source = staged.at[step]
        copy = remote(source, from_pair.at[step], pair_sems, step, axis, partner)
        copy.start()
        return copy

    pair, peer = {}, {}
    for step in order[:2]:
        pair[step] = send_pair(step)
    yield
    for index, step in enumerate(order[:-1]):
        other = lax.rem(me + 2 * step, amount)
        own = product(other)
        pair[step].wait_recv()
        staged_peer[step] = (own + from_pair[step].astype(jnp.float32)).astype(jnp.bfloat16)
        peer[step] = remote(
            staged_peer.at[step], from_peer.at[step], peer_sems, step, axis, other
        )
        peer[step].start()
        pair[step].wait_send()
        if index + 2 < half:
            pair[order[index + 2]] = send_pair(order[index + 2])
        yield
    own = product(me)
    pair[0].wait_recv()
    o_ref[...] = own + from_pair[0].astype(jnp.float32)
    yield
    for step in order[:-1]:
        peer[step].wait_recv()
        o_ref[...] += from_peer[step].astype(jnp.float32)
    pair[0].wait_send()
    for step in order[:-1]:
        peer[step].wait_send()


def exchange_kernel(plan, axes, *refs):
    refs = list(refs)
    take = lambda count: [refs.pop(0) for _ in range(count)]
    inputs = [take(2 if kind == "product" else 1) for kind, _, _, _ in plan]
    outputs = take(len(plan))
    running = []
    greet(axes)
    for (kind, axis, amount, weight_dim), ins, out in zip(plan, inputs, outputs):
        if kind == "gather":
            peer_sems, pair_sems, own_sem = take(2), take(2), take(1)[0]
            running.append(
                gather_steps(axis, amount, ins[0], out, peer_sems, pair_sems, own_sem)
            )
            continue
        staged = take(1)[0] if kind == "product" else None
        from_pair, staged_peer, from_peer = take(3)
        peer_sems, pair_sems = take(2), take(2)
        running.append(
            scatter_steps(
                axis,
                amount,
                weight_dim,
                ins[0],
                ins[1] if kind == "product" else None,
                out,
                staged,
                from_pair,
                staged_peer,
                from_peer,
                pair_sems,
                peer_sems,
            )
        )
    while running:
        still = []
        for one in running:
            if next(one, "end") != "end":
                still.append(one)
        running = still


def exchange(collective_id, *transfers):
    plan, axes, operands, results, scratch = [], {}, [], [], []
    for kind, axis, *arrays in transfers:
        amount = lax.axis_size(axis)
        half = amount // 2
        axes[axis] = amount
        weight_dim = arrays[2] if kind == "product" else None
        plan.append((kind, axis, amount, weight_dim))
        operand = arrays[0]
        sems = [pltpu.SemaphoreType.DMA((half,))] * 4
        if kind == "gather":
            operands.append(operand)
            results.append(jax.ShapeDtypeStruct((amount,) + operand.shape, operand.dtype))
            scratch += sems + [pltpu.SemaphoreType.DMA]
            continue
        if kind == "product":
            count = operand.shape[0] // amount
            width = arrays[1].shape[1 - weight_dim]
            operands += [operand.reshape(amount, count, operand.shape[1]), arrays[1]]
        else:
            count, width = operand.shape[1:]
            operands.append(operand)
        results.append(jax.ShapeDtypeStruct((count, width), jnp.float32))
        slots = pltpu.VMEM((half, count, width), jnp.bfloat16)
        scratch += [slots] * (4 if kind == "product" else 3) + sems
    return pl.pallas_call(
        functools.partial(exchange_kernel, tuple(plan), tuple(axes.items())),
        out_shape=results,
        in_specs=[pl.BlockSpec(memory_space=pltpu.VMEM)] * len(operands),
        out_specs=[pl.BlockSpec(memory_space=pltpu.VMEM)] * len(results),
        scratch_shapes=scratch,
        compiler_params=pltpu.CompilerParams(
            collective_id=collective_id, has_side_effects=True, vmem_limit_bytes=VMEM_GRANT
        ),
    )(*operands)


def pad_rows(rows, multiple):
    spare = -rows.shape[-2] % multiple
    return jnp.pad(rows, [(0, 0)] * (rows.ndim - 2) + [(0, spare), (0, 0)])


def join_columns(blocks, count):
    blocks = jnp.swapaxes(blocks[:, :count], 0, 1)
    return blocks.reshape(count, blocks.shape[1] * blocks.shape[2])


def cut_columns(whole, amount):
    count, width = whole.shape
    blocks = whole.astype(jnp.bfloat16).reshape(count, amount, width // amount)
    return pad_rows(jnp.swapaxes(blocks, 0, 1), 16)


def head_part(rows, head, scale=1.0):
    lane = lax.broadcasted_iota(jnp.int32, (1, rows.shape[1]), 1)
    inside = (lane >= head * HEAD_DIM) & (lane < (head + 1) * HEAD_DIM)
    return (rows.astype(jnp.float32) * jnp.where(inside, scale, 0.0)).astype(jnp.bfloat16)


def head_weights(query_part, key_rows, same_doc):
    scores = jnp.where(same_doc, contract_last(query_part, key_rows), MASKED)
    exp_scores = jnp.exp(scores - jnp.max(scores, axis=-1, keepdims=True))
    return exp_scores * (1.0 / jnp.sum(exp_scores, axis=-1, keepdims=True))


def attend_kernel(heads, q_ref, k_ref, v_ref, ids_ref, all_ids_ref, o_ref):
    same_doc = ids_ref[...] == all_ids_ref[...]
    total = None
    for head in range(heads):
        query_part = head_part(q_ref[...], head, HEAD_DIM**-0.5)
        weights = head_weights(query_part, k_ref[...], same_doc).astype(jnp.bfloat16)
        part = jnp.dot(weights, head_part(v_ref[...], head), preferred_element_type=jnp.float32)
        total = part if total is None else total + part
    o_ref[...] = total.astype(jnp.bfloat16)


def attend_back_kernel(
    heads, q_ref, k_ref, v_ref, ids_ref, all_ids_ref, g_ref, dq_ref, dk_ref, dv_ref
):
    @pl.when(pl.program_id(0) == 0)
    def _():
        dk_ref[...] = jnp.zeros_like(dk_ref)
        dv_ref[...] = jnp.zeros_like(dv_ref)

    same_doc = ids_ref[...] == all_ids_ref[...]
    total = None
    for head in range(heads):
        query_part = head_part(q_ref[...], head, HEAD_DIM**-0.5)
        grad_part = head_part(g_ref[...], head)
        weights = head_weights(query_part, k_ref[...], same_doc)
        dv_ref[...] += contract_first(weights.astype(jnp.bfloat16), grad_part)
        weight_grad = contract_last(grad_part, v_ref[...])
        delta = jnp.sum(weights * weight_grad, axis=-1, keepdims=True)
        score_grad = (weights * (weight_grad - delta)).astype(jnp.bfloat16)
        dk_ref[...] += contract_first(score_grad, query_part)
        part = jnp.dot(
            score_grad,
            head_part(k_ref[...], head, HEAD_DIM**-0.5),
            preferred_element_type=jnp.float32,
        )
        total = part if total is None else total + part
    dq_ref[...] = total


def attention(kernel, outs, queries, key_rows, values, doc_ids, *more):
    count, width = queries.shape
    block = min(256, count)
    rows = pl.BlockSpec((block, width), lambda index: (index, 0))
    whole = pl.BlockSpec((count, width), lambda index: (0, 0))
    return pl.pallas_call(
        functools.partial(kernel, width // HEAD_DIM),
        grid=(count // block,),
        out_shape=[jax.ShapeDtypeStruct((count, width), kind) for kind, _ in outs],
        in_specs=[
            rows,
            whole,
            whole,
            pl.BlockSpec((block, 1), lambda index: (index, 0)),
            pl.BlockSpec((1, count), lambda index: (0, 0)),
        ]
        + [rows] * len(more),
        out_specs=[rows if blocked else whole for _, blocked in outs],
        compiler_params=pltpu.CompilerParams(vmem_limit_bytes=VMEM_GRANT),
    )(queries, key_rows, values, doc_ids[:, None], doc_ids[None, :], *more)


def body(
    tokens,
    doc_lengths,
    attn_gain,
    qkv_weight,
    proj_weight,
    mlp_gain,
    in_weight,
    out_weight,
    cotangent,
):
    gains = lax.all_gather(jnp.stack([attn_gain, mlp_gain]), "dp", axis=1, tiled=True)
    attn_scale = gains[0].astype(jnp.float32)
    mlp_scale = gains[1].astype(jnp.float32)
    dp_size = lax.axis_size("dp")
    model_width = dp_size * qkv_weight.shape[0]
    local_width = qkv_weight.shape[2]
    local_heads = local_width // HEAD_DIM
    local_units = in_weight.shape[2]
    row_count = tokens.shape[0]
    group_rows = row_count * lax.axis_size("tensor")
    cosine, sine = rotary_tables(group_rows, HEAD_DIM)
    doc_ids = documents(doc_lengths[0], group_rows)
    inputs = tokens.astype(jnp.float32)
    plain_one, inverse_one = layer_norm(inputs)
    attn_normed = (plain_one * attn_scale).astype(jnp.bfloat16)
    attn_all, qkv_mat, in_mat, proj_blocks, out_blocks = exchange(
        1,
        ("gather", "tensor", attn_normed),
        ("gather", "dp", qkv_weight.reshape(-1, 3 * local_width)),
        ("gather", "dp", in_weight.reshape(-1, 2 * local_units)),
        ("gather", "dp", pad_rows(proj_weight, 16)),
        ("gather", "dp", pad_rows(out_weight, 16)),
    )
    attn_all = attn_all.reshape(group_rows, model_width)
    qkv_mat = qkv_mat.reshape(model_width, 3 * local_width)
    in_mat = in_mat.reshape(model_width, 2 * local_units)
    proj_local = join_columns(proj_blocks, local_width)
    out_rows = join_columns(out_blocks, local_units)
    qkv_rows = jnp.dot(attn_all, qkv_mat, preferred_element_type=jnp.float32).reshape(
        group_rows, 3, local_heads, HEAD_DIM
    )
    flat = (group_rows, local_width)
    queries = rotate(qkv_rows[:, 0], cosine, sine).astype(jnp.bfloat16).reshape(flat)
    key_rows = rotate(qkv_rows[:, 1], cosine, sine).astype(jnp.bfloat16).reshape(flat)
    values = qkv_rows[:, 2].astype(jnp.bfloat16).reshape(flat)
    attended = attention(
        attend_kernel, [(jnp.bfloat16, True)], queries, key_rows, values, doc_ids
    )[0]
    out_cot = cotangent.astype(jnp.float32)
    out_low = out_cot.astype(jnp.bfloat16)
    attn_branch, out_all = exchange(
        2, ("product", "tensor", attended, proj_local, 0), ("gather", "tensor", out_low)
    )
    out_all = out_all.reshape(group_rows, model_width)
    residual = inputs + attn_branch
    plain_two, inverse_two = layer_norm(residual)
    mlp_normed = (plain_two * mlp_scale).astype(jnp.bfloat16)
    mlp_all = exchange(3, ("gather", "tensor", mlp_normed))[0].reshape(group_rows, model_width)
    projected = jnp.dot(mlp_all, in_mat, preferred_element_type=jnp.float32)
    inner_part = projected[:, :local_units]
    gate_part = projected[:, local_units:]
    activated, gelu_pull = jax.vjp(exact_gelu, inner_part)
    hidden = (activated * gate_part).astype(jnp.bfloat16)
    out_weight_grad = contract_first(hidden, out_all)
    hidden_grad = contract_last(out_all, out_rows)
    inner_grad = gelu_pull(hidden_grad * gate_part)[0]
    gate_grad = hidden_grad * activated
    projected_grad = jnp.concatenate([inner_grad, gate_grad], axis=1).astype(jnp.bfloat16)
    in_weight_grad = contract_first(mlp_all, projected_grad).astype(jnp.bfloat16)
    mlp_normed_grad, mlp_branch, in_weight_sum, out_weight_sum = exchange(
        4,
        ("product", "tensor", projected_grad, in_mat, 1),
        ("product", "tensor", hidden, out_rows, 0),
        ("blocks", "dp", in_weight_grad.reshape(dp_size, -1, 2 * local_units)),
        ("blocks", "dp", cut_columns(out_weight_grad, dp_size)),
    )
    block_out = (residual + mlp_branch).astype(jnp.bfloat16)
    mlp_gain_part = jnp.sum(mlp_normed_grad * plain_two, axis=0)
    residual_grad = out_cot + norm_back(mlp_normed_grad * mlp_scale, plain_two, inverse_two)
    residual_low = residual_grad.astype(jnp.bfloat16)
    branch_all = exchange(5, ("gather", "tensor", residual_low))[0]
    branch_all = branch_all.reshape(group_rows, model_width)
    proj_weight_grad = contract_first(attended, branch_all)
    attended_grad = contract_last(branch_all, proj_local).astype(jnp.bfloat16)
    query_grad, key_grad, value_grad = attention(
        attend_back_kernel,
        [(jnp.float32, True), (jnp.float32, False), (jnp.float32, False)],
        queries,
        key_rows,
        values,
        doc_ids,
        attended_grad,
    )
    by_head = (group_rows, local_heads, HEAD_DIM)
    qkv_low_grad = jnp.concatenate(
        [
            unrotate(query_grad.reshape(by_head), cosine, sine).reshape(flat),
            unrotate(key_grad.reshape(by_head), cosine, sine).reshape(flat),
            value_grad,
        ],
        axis=1,
    ).astype(jnp.bfloat16)
    qkv_weight_grad = contract_first(attn_all, qkv_low_grad).astype(jnp.bfloat16)
    attn_normed_grad, qkv_weight_sum, proj_weight_sum = exchange(
        6,
        ("product", "tensor", qkv_low_grad, qkv_mat, 1),
        ("blocks", "dp", qkv_weight_grad.reshape(dp_size, -1, 3 * local_width)),
        ("blocks", "dp", cut_columns(proj_weight_grad, dp_size)),
    )
    attn_gain_part = jnp.sum(attn_normed_grad * plain_one, axis=0)
    tokens_grad = (
        residual_grad + norm_back(attn_normed_grad * attn_scale, plain_one, inverse_one)
    ).astype(jnp.bfloat16)
    gain_parts = jnp.pad(jnp.stack([attn_gain_part, mlp_gain_part]), ((0, 6), (0, 0)))
    gain_parts = jnp.sum(exchange(7, ("gather", "tensor", gain_parts))[0], axis=0)
    gain_parts = jnp.sum(exchange(8, ("gather", "dp", gain_parts))[0], axis=0)
    gain_width = attn_gain.shape[0]
    gain_grads = lax.dynamic_slice_in_dim(
        gain_parts, lax.axis_index("dp") * gain_width, gain_width, 1
    )
    return (
        block_out,
        tokens_grad,
        gain_grads[0],
        qkv_weight_sum.reshape(-1, 3, local_width),
        proj_weight_sum[:local_width],
        gain_grads[1],
        in_weight_sum.reshape(-1, 2, local_units),
        out_weight_sum[:local_units],
    )


def solution(mesh):
    in_specs = (
        P(("dp", "tensor"), None),
        P("dp", None),
        P("dp"),
        P("dp", None, "tensor"),
        P("tensor", "dp"),
        P("dp"),
        P("dp", None, "tensor"),
        P("tensor", "dp"),
        P(("dp", "tensor"), None),
    )
    out_specs = (
        P(("dp", "tensor"), None),
        P(("dp", "tensor"), None),
        P("dp"),
        P("dp", None, "tensor"),
        P("tensor", "dp"),
        P("dp"),
        P("dp", None, "tensor"),
        P("tensor", "dp"),
    )
    return jax.shard_map(body, mesh=mesh, in_specs=in_specs, out_specs=out_specs, check_vma=False)
```

```python
import functools
import math

import jax
import jax.numpy as jnp
from jax import lax
from jax.experimental import pallas as pl
from jax.experimental.pallas import tpu as pltpu
from jax.sharding import PartitionSpec as P

HEAD_DIM = 64


EPSILON = 1e-05
ROPE_BASE = 160000.0
MASKED = -1000000000.0


def layer_norm(values):
    centered = values - jnp.mean(values, axis=-1, keepdims=True)
    spread = jnp.mean(centered * centered, axis=-1, keepdims=True)
    inverse = lax.rsqrt(spread + EPSILON)
    return (centered * inverse, inverse)


def norm_back(scaled_grad, plain_rows, inverse):
    first_mean = jnp.mean(scaled_grad, axis=-1, keepdims=True)
    second_mean = jnp.mean(scaled_grad * plain_rows, axis=-1, keepdims=True)
    return inverse * (scaled_grad - first_mean - plain_rows * second_mean)


def rotary_tables(amount, head_width):
    half_width = head_width // 2
    frequency = jnp.exp(
        jnp.arange(half_width, dtype=jnp.float32) * (-2.0 * math.log(ROPE_BASE) / head_width)
    )
    angles = jnp.arange(amount, dtype=jnp.float32)[:, None] * frequency[None, :]
    return (jnp.cos(angles), jnp.sin(angles))


def rotate(values, cosine, sine):
    half_width = values.shape[-1] // 2
    lower_half = values[..., :half_width]
    upper_half = values[..., half_width:]
    cos_rows = cosine[:, None, :]
    sin_rows = sine[:, None, :]
    return jnp.concatenate(
        [
            lower_half * cos_rows - upper_half * sin_rows,
            upper_half * cos_rows + lower_half * sin_rows,
        ],
        axis=-1,
    )


def unrotate(gradient, cosine, sine):
    half_width = gradient.shape[-1] // 2
    lower_half = gradient[..., :half_width]
    upper_half = gradient[..., half_width:]
    cos_rows = cosine[:, None, :]
    sin_rows = sine[:, None, :]
    return jnp.concatenate(
        [
            lower_half * cos_rows + upper_half * sin_rows,
            upper_half * cos_rows - lower_half * sin_rows,
        ],
        axis=-1,
    )


def documents(lengths, amount):
    doc_ends = jnp.cumsum(lengths)
    positions = jnp.arange(amount, dtype=jnp.int32)
    return jnp.sum((positions[:, None] >= doc_ends[None, :]).astype(jnp.int32), axis=1)


def exact_gelu(values):
    return jax.nn.gelu(values, approximate=False)


def contract_last(left_side, right_side):
    return lax.dot_general(
        left_side, right_side, (((1,), (1,)), ((), ())), preferred_element_type=jnp.float32
    )


def contract_first(left_side, right_side):
    return lax.dot_general(
        left_side, right_side, (((0,), (0,)), ((), ())), preferred_element_type=jnp.float32
    )


VMEM_GRANT = 48 * 1024 * 1024


def remote(source, target, sems, step, axis, other):
    return pltpu.make_async_remote_copy(
        src_ref=source,
        dst_ref=target,
        send_sem=sems[0].at[step],
        recv_sem=sems[1].at[step],
        device_id={axis: other},
        device_id_type=pl.DeviceIdType.MESH,
    )


def place(axis, amount):
    me = lax.axis_index(axis)
    return (me, me + 1 - 2 * lax.rem(me, 2))


def greet(axes):
    barrier = pltpu.get_barrier_semaphore()
    total = 0
    for axis, amount in axes:
        me, partner = place(axis, amount)
        peers = [lax.rem(me + 2 * step, amount) for step in range(1, amount // 2)]
        for other in [partner] + peers:
            pl.semaphore_signal(
                barrier, inc=1, device_id={axis: other}, device_id_type=pl.DeviceIdType.MESH
            )
        total += amount // 2
    pl.semaphore_wait(barrier, total)


def steps_by_distance(half):
    return sorted(range(1, half), key=lambda step: min(step, half - step))


def gather_steps(axis, amount, x_ref, o_ref, right_sems, left_sems, pair_sems, own_sem):
    me, partner = place(axis, amount)
    last = amount // 2 - 1
    spot = lax.div(me, 2)

    def slot(base, step):
        return o_ref.at[lax.rem(base + 2 * step + amount, amount)]

    def hop(step, way, sems):
        origin = slot(me, -way * (step - 1))
        source = x_ref if step == 1 else origin
        other = lax.rem(me + 2 * way + amount, amount)
        return remote(source, origin, sems, step - 1, axis, other)

    def arrival(step, way, sems):
        origin = slot(me, -way * step)
        other = lax.rem(me + 2 * way + amount, amount)
        return remote(origin, origin, sems, step - 1, axis, other)

    def to_pair(index, step, base):
        origin = slot(base, step)
        source = x_ref if step == 0 and base is me else origin
        return remote(source, origin, pair_sems, index, axis, partner)

    ways = [(1, right_sems), (-1, left_sems)]

    def reached(step, way):
        return spot >= step if way == 1 else spot <= last - step

    def room(way):
        return spot < last if way == 1 else spot > 0

    def index_of(step, way):
        return step if way == 1 else last + step

    own = pltpu.make_async_copy(x_ref, o_ref.at[me], own_sem)
    own.start()
    for way, sems in ways:

        @pl.when(room(way))
        def _():
            hop(1, way, sems).start()

    to_pair(0, 0, me).start()
    yield
    for step in range(1, last + 1):
        for way, sems in ways:

            @pl.when(reached(step, way))
            def _():
                arrival(step, way, sems).wait_recv()

            if step < last:

                @pl.when(reached(step, way) & room(way))
                def _():
                    hop(step + 1, way, sems).start()

            @pl.when(reached(step, way))
            def _():
                to_pair(index_of(step, way), -way * step, me).start()

        yield
    to_pair(0, 0, partner).wait_recv()
    for step in range(1, last + 1):
        for way, sems in ways:

            @pl.when(reached(step, way))
            def _():
                to_pair(index_of(step, way), -way * step, partner).wait_recv()
                to_pair(index_of(step, way), -way * step, me).wait_send()

            @pl.when(reached(step - 1, way) & room(way))
            def _():
                hop(step, way, sems).wait_send()

    to_pair(0, 0, me).wait_send()
    own.wait()


def run(steps):
    for _ in steps:
        pass


def scatter_steps(
    axis,
    amount,
    weight_dim,
    a_ref,
    w_ref,
    o_ref,
    staged,
    from_pair,
    staged_peer,
    from_peer,
    pair_sems,
    peer_sems,
):
    me, partner = place(axis, amount)
    half = amount // 2
    order = steps_by_distance(half)[::-1] + [0]

    def product(chunk):
        if w_ref is None:
            return a_ref[chunk].astype(jnp.float32)
        return lax.dot_general(
            a_ref[chunk],
            w_ref[...],
            (((1,), (weight_dim,)), ((), ())),
            preferred_element_type=jnp.float32,
        )

    def send_pair(step):
        chunk = lax.rem(partner + 2 * step, amount)
        if w_ref is None:
            source = a_ref.at[chunk]
        else:
            staged[step] = product(chunk).astype(jnp.bfloat16)
            source = staged.at[step]
        copy = remote(source, from_pair.at[step], pair_sems, step, axis, partner)
        copy.start()
        return copy

    pair, peer = {}, {}
    for step in order[:2]:
        pair[step] = send_pair(step)
    yield
    for index, step in enumerate(order[:-1]):
        other = lax.rem(me + 2 * step, amount)
        own = product(other)
        pair[step].wait_recv()
        staged_peer[step] = (own + from_pair[step].astype(jnp.float32)).astype(jnp.bfloat16)
        peer[step] = remote(
            staged_peer.at[step], from_peer.at[step], peer_sems, step, axis, other
        )
        peer[step].start()
        pair[step].wait_send()
        if index + 2 < half:
            pair[order[index + 2]] = send_pair(order[index + 2])
        yield
    own = product(me)
    pair[0].wait_recv()
    o_ref[...] = own + from_pair[0].astype(jnp.float32)
    yield
    for step in order[:-1]:
        peer[step].wait_recv()
        o_ref[...] += from_peer[step].astype(jnp.float32)
    pair[0].wait_send()
    for step in order[:-1]:
        peer[step].wait_send()


def exchange_kernel(plan, axes, *refs):
    refs = list(refs)
    take = lambda count: [refs.pop(0) for _ in range(count)]
    amount_of = dict(axes)
    inputs = [take(INPUTS[kind]) for kind, _, _, _ in plan]
    outputs = [take(OUTPUTS[kind]) for kind, _, _, _ in plan]
    running = []
    greet(axes)

    def take_gather(axis, x_ref, o_ref):
        sems = [take(2), take(2), take(2), take(1)[0]]
        return gather_steps(axis, amount_of[axis], x_ref, o_ref, *sems)

    last = None
    for (kind, axis, amount, weight_dim), ins, outs in zip(plan, inputs, outputs):
        if kind == "gather":
            running.append(take_gather(axis, ins[0], outs[0]))
            continue
        if kind == "normed":
            x_ref, gain_ref = ins
            gain_slots, normed = take(2)
            run(take_gather("dp", gain_ref, gain_slots))
            outs[1][...] = jnp.sum(gain_slots[...].astype(jnp.float32), axis=0)
            plain_rows = layer_norm(x_ref[...].astype(jnp.float32))[0]
            normed[...] = (plain_rows * outs[1][0:1, :]).astype(jnp.bfloat16)
            running.append(take_gather(axis, normed, outs[0]))
            continue
        if kind == "gains":
            last = (ins, outs, take(4), take(14))
            continue
        staged = take(1)[0] if kind == "product" else None
        from_pair, staged_peer, from_peer = take(3)
        peer_sems, pair_sems = take(2), take(2)
        running.append(
            scatter_steps(
                axis,
                amount,
                weight_dim,
                ins[0],
                ins[1] if kind == "product" else None,
                outs[0],
                staged,
                from_pair,
                staged_peer,
                from_peer,
                pair_sems,
                peer_sems,
            )
        )
    while running:
        still = []
        for one in running:
            if next(one, "end") != "end":
                still.append(one)
        running = still
    if last is not None:
        (plain_ref, other_ref), outs, (rows, sums, tensor_slots, dp_slots), refs = last
        rows[...] = other_ref[...]
        rows[0:1, :] = jnp.sum(outputs[0][0][...] * plain_ref[...], axis=0, keepdims=True)
        run(take_gather("tensor", rows, tensor_slots))
        sums[...] = jnp.sum(tensor_slots[...], axis=0)
        run(take_gather("dp", sums, dp_slots))
        outs[0][...] = jnp.sum(dp_slots[...], axis=0)


INPUTS = {"gather": 1, "normed": 2, "gains": 2, "product": 2, "blocks": 1}
OUTPUTS = {"gather": 1, "normed": 2, "gains": 1, "product": 1, "blocks": 1}


def gather_sems(axis):
    half = lax.axis_size(axis) // 2
    line = [pltpu.SemaphoreType.DMA((max(half - 1, 1),))] * 4
    return line + [pltpu.SemaphoreType.DMA((2 * half - 1,))] * 2 + [pltpu.SemaphoreType.DMA]


def exchange(collective_id, *transfers):
    plan, axes, operands, results, scratch = [], {}, [], [], []
    for kind, axis, *arrays in transfers:
        amount = lax.axis_size(axis)
        half = amount // 2
        axes[axis] = amount
        weight_dim = arrays[2] if kind == "product" else None
        plan.append((kind, axis, amount, weight_dim))
        operand = arrays[0]
        if kind == "gather":
            operands.append(operand)
            results.append(jax.ShapeDtypeStruct((amount,) + operand.shape, operand.dtype))
            scratch += gather_sems(axis)
            continue
        if kind == "normed":
            operands += arrays
            gains = arrays[1]
            axes["dp"] = lax.axis_size("dp")
            results.append(jax.ShapeDtypeStruct((amount,) + operand.shape, operand.dtype))
            results.append(jax.ShapeDtypeStruct(gains.shape, jnp.float32))
            scratch.append(pltpu.VMEM((axes["dp"],) + gains.shape, gains.dtype))
            scratch.append(pltpu.VMEM(operand.shape, operand.dtype))
            scratch += gather_sems("dp") + gather_sems(axis)
            continue
        if kind == "gains":
            operands += arrays
            shape = arrays[1].shape
            axes["dp"] = lax.axis_size("dp")
            results.append(jax.ShapeDtypeStruct(shape, jnp.float32))
            scratch += [pltpu.VMEM(shape, jnp.float32)] * 2
            scratch.append(pltpu.VMEM((amount,) + shape, jnp.float32))
            scratch.append(pltpu.VMEM((axes["dp"],) + shape, jnp.float32))
            scratch += gather_sems(axis) + gather_sems("dp")
            continue
        sems = [pltpu.SemaphoreType.DMA((half,))] * 4
        if kind == "product":
            count = operand.shape[0] // amount
            width = arrays[1].shape[1 - weight_dim]
            operands += [operand.reshape(amount, count, operand.shape[1]), arrays[1]]
        else:
            count, width = operand.shape[1:]
            operands.append(operand)
        results.append(jax.ShapeDtypeStruct((count, width), jnp.float32))
        slots = pltpu.VMEM((half, count, width), jnp.bfloat16)
        scratch += [slots] * (4 if kind == "product" else 3) + sems
    return pl.pallas_call(
        functools.partial(exchange_kernel, tuple(plan), tuple(axes.items())),
        out_shape=results,
        in_specs=[pl.BlockSpec(memory_space=pltpu.VMEM)] * len(operands),
        out_specs=[pl.BlockSpec(memory_space=pltpu.VMEM)] * len(results),
        scratch_shapes=scratch,
        compiler_params=pltpu.CompilerParams(
            collective_id=collective_id, has_side_effects=True, vmem_limit_bytes=VMEM_GRANT
        ),
    )(*operands)


def pad_rows(rows, multiple):
    spare = -rows.shape[-2] % multiple
    return jnp.pad(rows, [(0, 0)] * (rows.ndim - 2) + [(0, spare), (0, 0)])


def join_columns(blocks, count):
    blocks = jnp.swapaxes(blocks[:, :count], 0, 1)
    return blocks.reshape(count, blocks.shape[1] * blocks.shape[2])


def cut_columns(whole, amount):
    count, width = whole.shape
    blocks = whole.astype(jnp.bfloat16).reshape(count, amount, width // amount)
    return pad_rows(jnp.swapaxes(blocks, 0, 1), 16)


def head_part(rows, head, scale=1.0):
    lane = lax.broadcasted_iota(jnp.int32, (1, rows.shape[1]), 1)
    inside = (lane >= head * HEAD_DIM) & (lane < (head + 1) * HEAD_DIM)
    return (rows.astype(jnp.float32) * jnp.where(inside, scale, 0.0)).astype(jnp.bfloat16)


def head_weights(query_part, key_rows, same_doc):
    scores = jnp.where(same_doc, contract_last(query_part, key_rows), MASKED)
    exp_scores = jnp.exp(scores - jnp.max(scores, axis=-1, keepdims=True))
    return exp_scores * (1.0 / jnp.sum(exp_scores, axis=-1, keepdims=True))


def attend_kernel(heads, q_ref, k_ref, v_ref, ids_ref, all_ids_ref, o_ref):
    same_doc = ids_ref[...] == all_ids_ref[...]
    total = None
    for head in range(heads):
        query_part = head_part(q_ref[...], head, HEAD_DIM**-0.5)
        weights = head_weights(query_part, k_ref[...], same_doc).astype(jnp.bfloat16)
        part = jnp.dot(weights, head_part(v_ref[...], head), preferred_element_type=jnp.float32)
        total = part if total is None else total + part
    o_ref[...] = total.astype(jnp.bfloat16)


def attend_back_kernel(
    heads, q_ref, k_ref, v_ref, ids_ref, all_ids_ref, g_ref, dq_ref, dk_ref, dv_ref
):
    @pl.when(pl.program_id(0) == 0)
    def _():
        dk_ref[...] = jnp.zeros_like(dk_ref)
        dv_ref[...] = jnp.zeros_like(dv_ref)

    same_doc = ids_ref[...] == all_ids_ref[...]
    total = None
    for head in range(heads):
        query_part = head_part(q_ref[...], head, HEAD_DIM**-0.5)
        grad_part = head_part(g_ref[...], head)
        weights = head_weights(query_part, k_ref[...], same_doc)
        dv_ref[...] += contract_first(weights.astype(jnp.bfloat16), grad_part)
        weight_grad = contract_last(grad_part, v_ref[...])
        delta = jnp.sum(weights * weight_grad, axis=-1, keepdims=True)
        score_grad = (weights * (weight_grad - delta)).astype(jnp.bfloat16)
        dk_ref[...] += contract_first(score_grad, query_part)
        part = jnp.dot(
            score_grad,
            head_part(k_ref[...], head, HEAD_DIM**-0.5),
            preferred_element_type=jnp.float32,
        )
        total = part if total is None else total + part
    dq_ref[...] = total


def attention(kernel, outs, queries, key_rows, values, doc_ids, *more):
    count, width = queries.shape
    block = min(256, count)
    rows = pl.BlockSpec((block, width), lambda index: (index, 0))
    whole = pl.BlockSpec((count, width), lambda index: (0, 0))
    return pl.pallas_call(
        functools.partial(kernel, width // HEAD_DIM),
        grid=(count // block,),
        out_shape=[jax.ShapeDtypeStruct((count, width), kind) for kind, _ in outs],
        in_specs=[
            rows,
            whole,
            whole,
            pl.BlockSpec((block, 1), lambda index: (index, 0)),
            pl.BlockSpec((1, count), lambda index: (0, 0)),
        ]
        + [rows] * len(more),
        out_specs=[rows if blocked else whole for _, blocked in outs],
        compiler_params=pltpu.CompilerParams(vmem_limit_bytes=VMEM_GRANT),
    )(queries, key_rows, values, doc_ids[:, None], doc_ids[None, :], *more)


def body(
    tokens,
    doc_lengths,
    attn_gain,
    qkv_weight,
    proj_weight,
    mlp_gain,
    in_weight,
    out_weight,
    cotangent,
):
    dp_size = lax.axis_size("dp")
    model_width = dp_size * qkv_weight.shape[0]
    local_width = qkv_weight.shape[2]
    local_heads = local_width // HEAD_DIM
    local_units = in_weight.shape[2]
    row_count = tokens.shape[0]
    group_rows = row_count * lax.axis_size("tensor")
    cosine, sine = rotary_tables(group_rows, HEAD_DIM)
    doc_ids = documents(doc_lengths[0], group_rows)
    inputs = tokens.astype(jnp.float32)
    plain_one, inverse_one = layer_norm(inputs)
    gain_width = attn_gain.shape[0]
    gain_rows = lax.dynamic_update_slice(
        jnp.zeros((16, model_width), jnp.bfloat16),
        jnp.stack([attn_gain, mlp_gain]),
        (0, lax.axis_index("dp") * gain_width),
    )
    attn_all, gains, qkv_mat, in_mat, proj_blocks, out_blocks = exchange(
        1,
        ("normed", "tensor", tokens, gain_rows),
        ("gather", "dp", qkv_weight.reshape(-1, 3 * local_width)),
        ("gather", "dp", in_weight.reshape(-1, 2 * local_units)),
        ("gather", "dp", pad_rows(proj_weight, 16)),
        ("gather", "dp", pad_rows(out_weight, 16)),
    )
    attn_scale, mlp_scale = gains[0], gains[1]
    attn_all = attn_all.reshape(group_rows, model_width)
    qkv_mat = qkv_mat.reshape(model_width, 3 * local_width)
    in_mat = in_mat.reshape(model_width, 2 * local_units)
    proj_local = join_columns(proj_blocks, local_width)
    out_rows = join_columns(out_blocks, local_units)
    qkv_rows = jnp.dot(attn_all, qkv_mat, preferred_element_type=jnp.float32).reshape(
        group_rows, 3, local_heads, HEAD_DIM
    )
    flat = (group_rows, local_width)
    queries = rotate(qkv_rows[:, 0], cosine, sine).astype(jnp.bfloat16).reshape(flat)
    key_rows = rotate(qkv_rows[:, 1], cosine, sine).astype(jnp.bfloat16).reshape(flat)
    values = qkv_rows[:, 2].astype(jnp.bfloat16).reshape(flat)
    attended = attention(
        attend_kernel, [(jnp.bfloat16, True)], queries, key_rows, values, doc_ids
    )[0]
    out_cot = cotangent.astype(jnp.float32)
    out_low = out_cot.astype(jnp.bfloat16)
    attn_branch, out_all = exchange(
        2, ("product", "tensor", attended, proj_local, 0), ("gather", "tensor", out_low)
    )
    out_all = out_all.reshape(group_rows, model_width)
    residual = inputs + attn_branch
    plain_two, inverse_two = layer_norm(residual)
    mlp_normed = (plain_two * mlp_scale).astype(jnp.bfloat16)
    mlp_all = exchange(3, ("gather", "tensor", mlp_normed))[0].reshape(group_rows, model_width)
    projected = jnp.dot(mlp_all, in_mat, preferred_element_type=jnp.float32)
    inner_part = projected[:, :local_units]
    gate_part = projected[:, local_units:]
    activated, gelu_pull = jax.vjp(exact_gelu, inner_part)
    hidden = (activated * gate_part).astype(jnp.bfloat16)
    out_weight_grad = contract_first(hidden, out_all)
    hidden_grad = contract_last(out_all, out_rows)
    inner_grad = gelu_pull(hidden_grad * gate_part)[0]
    gate_grad = hidden_grad * activated
    projected_grad = jnp.concatenate([inner_grad, gate_grad], axis=1).astype(jnp.bfloat16)
    in_weight_grad = contract_first(mlp_all, projected_grad).astype(jnp.bfloat16)
    mlp_normed_grad, mlp_branch, in_weight_sum, out_weight_sum = exchange(
        4,
        ("product", "tensor", projected_grad, in_mat, 1),
        ("product", "tensor", hidden, out_rows, 0),
        ("blocks", "dp", in_weight_grad.reshape(dp_size, -1, 2 * local_units)),
        ("blocks", "dp", cut_columns(out_weight_grad, dp_size)),
    )
    block_out = (residual + mlp_branch).astype(jnp.bfloat16)
    mlp_gain_part = jnp.sum(mlp_normed_grad * plain_two, axis=0)
    residual_grad = out_cot + norm_back(mlp_normed_grad * mlp_scale, plain_two, inverse_two)
    residual_low = residual_grad.astype(jnp.bfloat16)
    branch_all = exchange(5, ("gather", "tensor", residual_low))[0]
    branch_all = branch_all.reshape(group_rows, model_width)
    proj_weight_grad = contract_first(attended, branch_all)
    attended_grad = contract_last(branch_all, proj_local).astype(jnp.bfloat16)
    query_grad, key_grad, value_grad = attention(
        attend_back_kernel,
        [(jnp.float32, True), (jnp.float32, False), (jnp.float32, False)],
        queries,
        key_rows,
        values,
        doc_ids,
        attended_grad,
    )
    by_head = (group_rows, local_heads, HEAD_DIM)
    qkv_low_grad = jnp.concatenate(
        [
            unrotate(query_grad.reshape(by_head), cosine, sine).reshape(flat),
            unrotate(key_grad.reshape(by_head), cosine, sine).reshape(flat),
            value_grad,
        ],
        axis=1,
    ).astype(jnp.bfloat16)
    qkv_weight_grad = contract_first(attn_all, qkv_low_grad).astype(jnp.bfloat16)
    other_gain = jnp.pad(mlp_gain_part[None, :], ((1, 6), (0, 0)))
    attn_normed_grad, qkv_weight_sum, proj_weight_sum, gain_parts = exchange(
        6,
        ("product", "tensor", qkv_low_grad, qkv_mat, 1),
        ("blocks", "dp", qkv_weight_grad.reshape(dp_size, -1, 3 * local_width)),
        ("blocks", "dp", cut_columns(proj_weight_grad, dp_size)),
        ("gains", "tensor", plain_one, other_gain),
    )
    tokens_grad = (
        residual_grad + norm_back(attn_normed_grad * attn_scale, plain_one, inverse_one)
    ).astype(jnp.bfloat16)
    gain_grads = lax.dynamic_slice_in_dim(
        gain_parts, lax.axis_index("dp") * gain_width, gain_width, 1
    )
    return (
        block_out,
        tokens_grad,
        gain_grads[0],
        qkv_weight_sum.reshape(-1, 3, local_width),
        proj_weight_sum[:local_width],
        gain_grads[1],
        in_weight_sum.reshape(-1, 2, local_units),
        out_weight_sum[:local_units],
    )


def solution(mesh):
    in_specs = (
        P(("dp", "tensor"), None),
        P("dp", None),
        P("dp"),
        P("dp", None, "tensor"),
        P("tensor", "dp"),
        P("dp"),
        P("dp", None, "tensor"),
        P("tensor", "dp"),
        P(("dp", "tensor"), None),
    )
    out_specs = (
        P(("dp", "tensor"), None),
        P(("dp", "tensor"), None),
        P("dp"),
        P("dp", None, "tensor"),
        P("tensor", "dp"),
        P("dp"),
        P("dp", None, "tensor"),
        P("tensor", "dp"),
    )
    return jax.shard_map(body, mesh=mesh, in_specs=in_specs, out_specs=out_specs, check_vma=False)
```
